32 devices in a mesh: lat: 16 (over z, x, core), lev: 2 (over y).
Axes of the slice: x: 2, y: 2, z: 4, core: 2. Of those that a mesh axis runs over, the one named last changes fastest.
Arguments:
- zonal_wind: float32 [8, 256, 2880], P('lev', 'lat'), may hold values from -6 to 6
- merid_wind: float32 [8, 256, 2880], P('lev', 'lat'), may hold values from -6 to 6
- tracer: float32 [8, 256, 2880], P('lev', 'lat'), may hold values from -6 to 6
- vertical_wind: float32 [8, 256, 2880], P('lev', 'lat'), may hold values from -6 to 6
- cutoff: int32 [256], replicated, may hold values from 1 to 1440, as said below
Outputs:
- zonal_next: float32 [8, 256, 2880], P('lev', 'lat')
- merid_next: float32 [8, 256, 2880], P('lev', 'lat')
- tracer_next: float32 [8, 256, 2880], P('lev', 'lat')
The draws below stay inside these ranges and needn't reach their ends.
Inputs may be any that keep to these rules, and one draw needn't show every extreme that they name: With d the distance of latitude j in rows from the nearer pole (d = 1 for the first and last latitude): cutoff is 1 at d = 1, 719 at d = 40, between 1 and 719 for d < 40, and 1440 for d > 40.
All inputs are finite; a program needn't handle non-finite values.
Results may differ from the reference program's by a relative error of at most 0.0001.
Values sent between devices are 32-bit elements; how exact they have to be, the bound alone decides.
A program may use at most 128 MiB of HBM per device.

```python
import math
import jax
import jax.numpy as jnp
from jax import lax

NLON = 2880
KMAX = 720
NLAT = 256
LEVELS = 8
CAP = 40


def draw_cutoff(key, part):
    row_ids = jnp.arange(NLAT, dtype=jnp.int32)
    depths = jnp.minimum(row_ids, NLAT - 1 - row_ids) + 1
    base_step = max(KMAX // CAP, 1)
    slopes = jax.random.randint(key, (NLAT,), max(base_step // 2, 1), 2 * base_step + 1, dtype=jnp.int32)
    rising = jnp.minimum(1 + (depths - 1) * slopes, KMAX - 1)
    rising = jnp.where(depths == CAP, KMAX - 1, rising)
    return jnp.where(depths <= CAP, rising, NLON // 2).astype(jnp.int32)


def block_levels(rng, extent, split, least, largest):
    factor_of, own = 1.0, jax.random.fold_in(rng, 6)
    for position, parts in split:
        draws = jnp.exp(jax.random.uniform(jax.random.fold_in(own, position), (parts,), jnp.float32, least / len(split), largest / len(split)))
        factor_of = factor_of * jnp.repeat(draws, extent[position] // parts).reshape([-1 if axis == position else 1 for axis in range(len(extent))])
    return factor_of


def bell_draw(rng, extent, width, bound, pieces=(), kind=jnp.bfloat16):
    values = jax.random.normal(rng, extent, jnp.float32) * width
    if len(pieces) > 0:
        values = block_levels(rng, extent, pieces, -0.22, 0.18) * values
    return jnp.clip(values, min=-bound, max=bound).astype(kind)


def setup_inputs(seed: int = 0) -> dict:
    keys = jax.random.split(jax.random.key(seed), 6)
    return {
        "zonal_wind": bell_draw(keys[0], (LEVELS, NLAT, NLON), 1.0, 6.0, ((0, 2), (1, 16)), jnp.float32),
        "merid_wind": bell_draw(keys[1], (LEVELS, NLAT, NLON), 1.0, 6.0, ((0, 2), (1, 16)), jnp.float32),
        "tracer": bell_draw(keys[2], (LEVELS, NLAT, NLON), 1.0, 6.0, ((0, 2), (1, 16)), jnp.float32),
        "vertical_wind": bell_draw(keys[3], (LEVELS, NLAT, NLON), 1.0, 6.0, ((0, 2), (1, 16)), jnp.float32),
        "cutoff": draw_cutoff(jax.random.fold_in(keys[5], 71), 0),
    }


zonal_scale = 0.1
merid_scale = 0.1
vertical_scale = 0.1
highest = lax.Precision.HIGHEST


def mode_tables(first_mode, mode_count):
    point_ids = jnp.arange(NLON, dtype=jnp.int32)
    mode_ids = first_mode + jnp.arange(mode_count, dtype=jnp.int32)
    phase_ids = (point_ids[:, None] * mode_ids[None, :]) % NLON
    angles = phase_ids.astype(jnp.float32) * (2.0 * math.pi / NLON)
    return jnp.cos(angles), jnp.sin(angles)


def mode_weights(cut_rows, first_mode, mode_count):
    mode_ids = first_mode + jnp.arange(mode_count, dtype=jnp.int32)
    factor = jnp.where(mode_ids == 0, jnp.float32(1.0), jnp.float32(2.0)) / NLON
    return jnp.where(mode_ids[None, :] <= cut_rows[:, None], factor[None, :], jnp.float32(0.0))


def lowpass(fields, cut_rows, tables):
    summed = jnp.zeros_like(fields)
    for first_mode, cosines, sines in tables:
        weight = mode_weights(cut_rows, first_mode, cosines.shape[1])
        cosine_part = jnp.einsum("flan,nk->flak", fields, cosines, precision=highest, preferred_element_type=jnp.float32) * weight[None, None]
        sine_part = jnp.einsum("flan,nk->flak", fields, sines, precision=highest, preferred_element_type=jnp.float32) * weight[None, None]
        summed = summed + jnp.einsum("flak,nk->flan", cosine_part, cosines, precision=highest, preferred_element_type=jnp.float32)
        summed = summed + jnp.einsum("flak,nk->flan", sine_part, sines, precision=highest, preferred_element_type=jnp.float32)
    filtered_mask = (cut_rows < NLON // 2)[None, None, :, None]
    return jnp.where(filtered_mask, summed, fields)


def advect(field, zonal, merid, vertical):
    lat_rows = field.shape[1]
    east_wind = 0.5 * (zonal + jnp.roll(zonal, -1, axis=2))
    flux_x = zonal_scale * east_wind * (0.5 * (field + jnp.roll(field, -1, axis=2)))
    div_x = flux_x - jnp.roll(flux_x, 1, axis=2)
    face_ids = jnp.arange(lat_rows + 1, dtype=jnp.int32).astype(jnp.float32)
    face_cos = jnp.sin(face_ids * (math.pi / lat_rows))
    center_ids = jnp.arange(lat_rows, dtype=jnp.int32).astype(jnp.float32)
    center_cos = jnp.sin((center_ids + 0.5) * (math.pi / lat_rows))
    merid_lat = jnp.pad(merid, ((0, 0), (1, 1), (0, 0)))
    field_lat = jnp.pad(field, ((0, 0), (1, 1), (0, 0)))
    north_wind = 0.5 * (merid_lat[:, :-1] + merid_lat[:, 1:])
    flux_y = merid_scale * face_cos[None, :, None] * north_wind * (0.5 * (field_lat[:, :-1] + field_lat[:, 1:]))
    div_y = flux_y[:, 1:] - flux_y[:, :-1]
    vertical_pad = jnp.pad(vertical, ((1, 1), (0, 0), (0, 0)))
    field_lev = jnp.pad(field, ((1, 1), (0, 0), (0, 0)))
    upward = 0.5 * (vertical_pad[:-1] + vertical_pad[1:])
    flux_z = vertical_scale * upward * (0.5 * (field_lev[:-1] + field_lev[1:]))
    div_z = flux_z[1:] - flux_z[:-1]
    return field - (div_x + div_y) / center_cos[None, :, None] - div_z


def reference(zonal_wind, merid_wind, tracer, vertical_wind, cutoff):
    cosines, sines = mode_tables(0, KMAX)
    tables = [(0, cosines, sines)]
    stacked = jnp.stack([zonal_wind, merid_wind, tracer])
    south_rows = lowpass(stacked[:, :, :CAP], cutoff[:CAP], tables)
    north_rows = lowpass(stacked[:, :, NLAT - CAP:], cutoff[NLAT - CAP:], tables)
    filtered = jnp.concatenate([south_rows, stacked[:, :, CAP:NLAT - CAP], north_rows], axis=2)
    zonal_next = advect(filtered[0], filtered[0], filtered[1], vertical_wind)
    merid_next = advect(filtered[1], filtered[0], filtered[1], vertical_wind)
    tracer_next = advect(filtered[2], filtered[0], filtered[1], vertical_wind)
    return (zonal_next, merid_next, tracer_next)
```

```python
import math

import jax
import jax.numpy as jnp
import ml_dtypes
import numpy as np
from jax import lax
from jax.experimental import pallas as pl
from jax.experimental.pallas import tpu as pltpu
from jax.sharding import PartitionSpec as P

NLON = 2880
KMAX = 720
HALF = NLON // 2
CHUNK = 128
MESH = pl.DeviceIdType.MESH
QUARTER = 0.025


def half_tables():
    modes = KMAX // 2
    chunks = -(-modes // CHUNK)
    tables = np.zeros((2, chunks, HALF, 2 * CHUNK), np.float32)
    points = np.arange(HALF, dtype=np.int64)
    for parity in range(2):
        for chunk in range(chunks):
            ids = np.arange(chunk * CHUNK, min((chunk + 1) * CHUNK, modes), dtype=np.int64)
            angles = (points[:, None] * (2 * ids + parity)[None, :] % NLON) * (2.0 * math.pi / NLON)
            tables[parity, chunk, :, : len(ids)] = np.cos(angles)
            tables[parity, chunk, :, CHUNK : CHUNK + len(ids)] = np.sin(angles)
    tables = tables.reshape(2 * chunks, HALF, 2 * CHUNK)
    high = tables.astype(ml_dtypes.bfloat16)
    low = (tables - high.astype(np.float32)).astype(ml_dtypes.bfloat16)
    return high, low


def split(x):
    high = x.astype(jnp.bfloat16)
    return high, (x - high.astype(jnp.float32)).astype(jnp.bfloat16)


def dot(a, b, transposed=False):
    dims = (((1,), (1 if transposed else 0,)), ((), ()))
    return lax.dot_general(a, b, dims, preferred_element_type=jnp.float32)


def filter_kernel(chunks, flag_ref, zonal, merid, tracer, cut_ref, high_ref, low_ref, out_ref, xh, xl, acc):
    step = pl.program_id(0)
    steps = 2 * chunks
    parity = step // chunks
    chunk = step % chunks
    fields = (zonal, merid, tracer)
    levels, lat_rows = zonal.shape[0], zonal.shape[1]
    rows = levels * lat_rows
    active = flag_ref[0] > 0

    @pl.when(jnp.logical_and(step == 0, jnp.logical_not(active)))
    def _():
        for f in range(3):
            out_ref[f] = fields[f][...]

    @pl.when(jnp.logical_and(step == 0, active))
    def _():
        for f in range(3):
            for l in range(levels):
                x = fields[f][l]
                first, second = x[:, :HALF], x[:, HALF:]
                at = pl.ds(f * rows + l * lat_rows, lat_rows)
                for p, folded in enumerate((first + second, first - second)):
                    high, low = split(folded)
                    xh[p, at, :] = high
                    xl[p, at, :] = low

    @pl.when(active)
    def _():
        th, tl = high_ref[0], low_ref[0]
        spectrum = dot(xh[parity], th) + dot(xl[parity], th) + dot(xh[parity], tl)
        lane = lax.broadcasted_iota(jnp.int32, spectrum.shape, 1) % CHUNK
        mode = 2 * (chunk * CHUNK + lane) + parity
        factor = jnp.where(mode == 0, jnp.float32(1.0 / NLON), jnp.float32(2.0 / NLON))
        spectrum = jnp.where(mode <= cut_ref[...], spectrum * factor, 0.0)
        sh, sl = split(spectrum)
        part = dot(sh, th, True) + dot(sl, th, True) + dot(sh, tl, True)

        @pl.when(chunk == 0)
        def _():
            acc[parity] = part

        @pl.when(chunk > 0)
        def _():
            acc[parity] += part

    @pl.when(jnp.logical_and(step == steps - 1, active))
    def _():
        for f in range(3):
            for l in range(levels):
                at = pl.ds(f * rows + l * lat_rows, lat_rows)
                keep = cut_ref[at, :] < HALF
                even, odd = acc[0, at, :], acc[1, at, :]
                y = jnp.concatenate([even + odd, even - odd], axis=1)
                out_ref[f, l] = jnp.where(keep, y, fields[f][l])


def filtered_fields(zonal, merid, tracer, own_cut):
    high, low = half_tables()
    steps = high.shape[0]
    levels, lat_rows, _ = zonal.shape
    rows = 3 * levels * lat_rows
    flag = jnp.any(own_cut < HALF).astype(jnp.int32)[None]
    cuts = jnp.tile(own_cut, 3 * levels)[:, None]
    whole = pl.BlockSpec((levels, lat_rows, NLON), lambda i, flag: (0, 0, 0))
    table = pl.BlockSpec((1, HALF, 2 * CHUNK), lambda i, flag: (i * flag[0], 0, 0))
    return pl.pallas_call(
        lambda *refs: filter_kernel(steps // 2, *refs),
        out_shape=jax.ShapeDtypeStruct((3, levels, lat_rows, NLON), jnp.float32),
        grid_spec=pltpu.PrefetchScalarGridSpec(
            num_scalar_prefetch=1,
            grid=(steps,),
            in_specs=[whole, whole, whole, pl.BlockSpec((rows, 1), lambda i, flag: (0, 0)), table, table],
            out_specs=pl.BlockSpec((3, levels, lat_rows, NLON), lambda i, flag: (0, 0, 0, 0)),
            scratch_shapes=[
                pltpu.VMEM((2, rows, HALF), jnp.bfloat16),
                pltpu.VMEM((2, rows, HALF), jnp.bfloat16),
                pltpu.VMEM((2, rows, HALF), jnp.float32),
            ],
        ),
        compiler_params=pltpu.CompilerParams(vmem_limit_bytes=40 * 1024 * 1024),
    )(flag, zonal, merid, tracer, cuts, jnp.asarray(high), jnp.asarray(low))


def latitude_factors(total_rows):
    ids = np.arange(total_rows + 1, dtype=np.float64)
    face = np.sin(ids * (math.pi / total_rows))
    center = np.sin((ids[:-1] + 0.5) * (math.pi / total_rows))
    return np.stack(
        [QUARTER * face[:-1] / center, QUARTER * face[1:] / center, QUARTER / center], axis=1
    ).astype(np.float32)


def east_of(x):
    return jnp.concatenate([x[:, 1:], x[:, :1]], axis=1)


def west_of(x):
    return jnp.concatenate([x[:, -1:], x[:, :-1]], axis=1)


def advect_kernel(
    lat_count, lev_count, field_ref, wind_ref, factor_ref,
    out0, out1, out2, lev_field, lev_wind, lat_out, lat_in, send_sem, recv_sem,
):
    lat, lev = lax.axis_index("lat"), lax.axis_index("lev")
    outs = (out0, out1, out2)
    levels, lat_rows = wind_ref.shape[0], wind_ref.shape[1]
    has = (lev > 0, lev < lev_count - 1, lat > 0, lat < lat_count - 1)
    there = ((lat, lev - 1), (lat, lev + 1), (lat - 1, lev), (lat + 1, lev))

    barrier = pltpu.get_barrier_semaphore()
    for side in range(4):
        @pl.when(has[side])
        def _():
            pl.semaphore_signal(barrier, inc=1, device_id=there[side], device_id_type=MESH)

    for f in range(3):
        for l in range(levels):
            lat_out[0, f * levels + l : f * levels + l + 1, :] = field_ref[f, l, 0:1, :]
            lat_out[1, f * levels + l : f * levels + l + 1, :] = field_ref[f, l, lat_rows - 1 : lat_rows, :]
    pl.semaphore_wait(barrier, sum(side.astype(jnp.int32) for side in has))

    def remote(slot, source, target, to):
        return pltpu.make_async_remote_copy(
            src_ref=source, dst_ref=target, send_sem=send_sem.at[slot], recv_sem=recv_sem.at[slot],
            device_id=there[to], device_id_type=MESH,
        )

    lats = (
        (remote(4, lat_out.at[1], lat_in.at[0], 3), 3, 2),
        (remote(5, lat_out.at[0], lat_in.at[1], 2), 2, 3),
    )
    levs = (
        (remote(2, wind_ref.at[levels - 1], lev_wind.at[0], 1), 1, 0),
        (remote(3, wind_ref.at[0], lev_wind.at[1], 0), 0, 1),
        (remote(0, field_ref.at[:, levels - 1], lev_field.at[0], 1), 1, 0),
        (remote(1, field_ref.at[:, 0], lev_field.at[1], 0), 0, 1),
    )
    for copy, to, _ in lats + levs:
        pl.when(has[to])(copy.start)

    for side in range(2):
        @pl.when(jnp.logical_not(has[side]))
        def _():
            lev_field[side] = jnp.zeros(lev_field.shape[1:], jnp.float32)
            lev_wind[side] = jnp.zeros(lev_wind.shape[1:], jnp.float32)

        @pl.when(jnp.logical_not(has[2 + side]))
        def _():
            lat_in[side] = jnp.zeros(lat_in.shape[1:], jnp.float32)

    factors = factor_ref[pl.ds(pl.multiple_of(lat * lat_rows, lat_rows), lat_rows), :]
    row = lax.broadcasted_iota(jnp.int32, (lat_rows, 1), 0)
    low_face = jnp.where(row > 0, factors[:, 0:1], 0.0)
    high_face = jnp.where(row < lat_rows - 1, factors[:, 1:2], 0.0)
    zonal_factor = factors[:, 2:3]

    def inner(l, carry):
        below, above = jnp.maximum(l - 1, 0), jnp.minimum(l + 1, levels - 1)
        zonal = field_ref[0, l]
        merid = field_ref[1, l]
        wind_here = wind_ref[l]
        east_wind = (zonal + east_of(zonal)) * zonal_factor
        merid_pair = merid + jnp.roll(merid, 1, axis=0)
        low_wind = jnp.where(l > 0, jnp.float32(QUARTER), 0.0) * (wind_ref[below] + wind_here)
        high_wind = jnp.where(l < levels - 1, jnp.float32(QUARTER), 0.0) * (wind_here + wind_ref[above])
        for f in range(3):
            x = field_ref[f, l]
            flux_x = east_wind * (x + east_of(x))
            flux_y = merid_pair * (x + jnp.roll(x, 1, axis=0))
            div_y = high_face * jnp.roll(flux_y, -1, axis=0) - low_face * flux_y
            div_z = high_wind * (x + field_ref[f, above]) - low_wind * (field_ref[f, below] + x)
            outs[f][l] = x - (flux_x - west_of(flux_x)) - div_y - div_z
        return carry

    lax.fori_loop(0, levels, inner, 0)

    for copy, to, source in lats:
        pl.when(has[source])(copy.wait_recv)
    for side, at, factor in ((0, 0, factors[0:1, 0:1]), (1, lat_rows - 1, -factors[lat_rows - 1 :, 1:2])):
        for l in range(levels):
            own = pl.ds(at, 1)
            pair = factor * (lat_in[side, levels + l : levels + l + 1, :] + field_ref[1, l, own, :])
            for f in range(3):
                halo = lat_in[side, f * levels + l : f * levels + l + 1, :]
                outs[f][l, own, :] += pair * (halo + field_ref[f, l, own, :])

    for copy, to, source in levs:
        pl.when(has[source])(copy.wait_recv)
    for side, l, sign in ((0, 0, QUARTER), (1, levels - 1, -QUARTER)):
        pair = sign * (lev_wind[side] + wind_ref[l])
        for f in range(3):
            outs[f][l] += pair * (lev_field[side, f] + field_ref[f, l])
    for copy, to, _ in lats + levs:
        pl.when(has[to])(copy.wait_send)


def advected(fields, wind, lat_count, lev_count):
    levels, lat_rows, _ = wind.shape
    vmem = pl.BlockSpec(memory_space=pltpu.VMEM)
    one = jax.ShapeDtypeStruct(wind.shape, jnp.float32)
    return pl.pallas_call(
        lambda *refs: advect_kernel(lat_count, lev_count, *refs),
        out_shape=(one, one, one),
        in_specs=[vmem] * 3,
        out_specs=(vmem,) * 3,
        scratch_shapes=[
            pltpu.VMEM((2, 3, lat_rows, NLON), jnp.float32),
            pltpu.VMEM((2, lat_rows, NLON), jnp.float32),
            pltpu.VMEM((2, 3 * levels, NLON), jnp.float32),
            pltpu.VMEM((2, 3 * levels, NLON), jnp.float32),
            pltpu.SemaphoreType.DMA((6,)),
            pltpu.SemaphoreType.DMA((6,)),
        ],
        compiler_params=pltpu.CompilerParams(
            collective_id=0, has_side_effects=True, vmem_limit_bytes=32 * 1024 * 1024
        ),
    )(fields, wind, jnp.asarray(latitude_factors(lat_rows * lat_count)))


def solution(mesh):
    lat_count, lev_count = mesh.shape["lat"], mesh.shape["lev"]

    def on_device(zonal_wind, merid_wind, tracer, vertical_wind, cutoff):
        lat_rows = zonal_wind.shape[1]
        own_cut = lax.dynamic_slice_in_dim(cutoff, lax.axis_index("lat") * lat_rows, lat_rows)
        fields = filtered_fields(zonal_wind, merid_wind, tracer, own_cut)
        return advected(fields, vertical_wind, lat_count, lev_count)

    spec = P("lev", "lat", None)
    return jax.shard_map(
        on_device, mesh=mesh, in_specs=(spec,) * 4 + (P(),), out_specs=(spec,) * 3, check_vma=False
    )
```

```python
import math

import jax
import jax.numpy as jnp
import ml_dtypes
import numpy as np
from jax import lax
from jax.experimental import pallas as pl
from jax.experimental.pallas import tpu as pltpu
from jax.sharding import PartitionSpec as P

NLON = 2880
KMAX = 720
HALF = NLON // 2
CHUNK = 128
MESH = pl.DeviceIdType.MESH
QUARTER = 0.025


def half_tables():
    modes = KMAX // 2
    chunks = -(-modes // CHUNK)
    tables = np.zeros((2, chunks, HALF, 2 * CHUNK), np.float32)
    points = np.arange(HALF, dtype=np.int64)
    for parity in range(2):
        for chunk in range(chunks):
            ids = np.arange(chunk * CHUNK, min((chunk + 1) * CHUNK, modes), dtype=np.int64)
            angles = (points[:, None] * (2 * ids + parity)[None, :] % NLON) * (2.0 * math.pi / NLON)
            tables[parity, chunk, :, : len(ids)] = np.cos(angles)
            tables[parity, chunk, :, CHUNK : CHUNK + len(ids)] = np.sin(angles)
    tables = tables.reshape(2 * chunks, HALF, 2 * CHUNK)
    high = tables.astype(ml_dtypes.bfloat16)
    low = (tables - high.astype(np.float32)).astype(ml_dtypes.bfloat16)
    return high, low


def split(x):
    high = x.astype(jnp.bfloat16)
    return high, (x - high.astype(jnp.float32)).astype(jnp.bfloat16)


def dot(a, b, transposed=False):
    dims = (((1,), (1 if transposed else 0,)), ((), ()))
    return lax.dot_general(a, b, dims, preferred_element_type=jnp.float32)


def latitude_factors(total_rows):
    ids = np.arange(total_rows + 1, dtype=np.float64)
    face = np.sin(ids * (math.pi / total_rows))
    center = np.sin((ids[:-1] + 0.5) * (math.pi / total_rows))
    return np.stack(
        [QUARTER * face[:-1] / center, QUARTER * face[1:] / center, QUARTER / center], axis=1
    ).astype(np.float32)


def east_of(x):
    return jnp.concatenate([x[:, 1:], x[:, :1]], axis=1)


def west_of(x):
    return jnp.concatenate([x[:, -1:], x[:, :-1]], axis=1)


def kernel(
    lat_count, lev_count, cap, zonal_in, merid_in, tracer_in, wind_in, cut_ref, factor_ref, high_in, low_in,
    out0, out1, out2,
    field_ref, wind_ref, high_ref, low_ref, xh, xl, spec, spec_in, sh, sl, acc,
    lev_field, lev_wind, lat_out, lat_in,
    load_sem, table_sem, wind_send, wind_recv, raw_send, raw_recv, spec_send, spec_recv, lat_send, lat_recv,
):
    lat, lev = lax.axis_index("lat"), lax.axis_index("lev")
    inputs = (zonal_in, merid_in, tracer_in)
    outs = (out0, out1, out2)
    levels, lat_rows = wind_ref.shape[0], wind_ref.shape[1]
    steps = high_ref.shape[0]
    chunks = steps // 2
    edge = 3 * lat_rows
    rows = levels * edge
    half = lat_rows // 2
    total_rows = lat_count * lat_rows
    has = (lev > 0, lev < lev_count - 1, lat > 0, lat < lat_count - 1)
    there = ((lat, lev - 1), (lat, lev + 1), (lat - 1, lev), (lat + 1, lev))
    slots = 1 if lev_count == 2 else 2
    slot_of = (0, slots - 1)
    first_row = lat * lat_rows

    def spans(start, count):
        some = jnp.logical_or(start < cap, start + count > total_rows - cap)
        inside = jnp.logical_and(start + count > cap, start < total_rows - cap)
        return some, inside

    filtered, _ = spans(first_row, lat_rows)
    raw = tuple(spans(first_row + h * half, half)[1] for h in range(2))

    barrier = pltpu.get_barrier_semaphore()
    for side in range(4):
        @pl.when(has[side])
        def _():
            pl.semaphore_signal(barrier, inc=1, device_id=there[side], device_id_type=MESH)

    loads = [pltpu.make_async_copy(inputs[f], field_ref.at[f], load_sem.at[f]) for f in range(3)]
    load_wind = pltpu.make_async_copy(wind_in, wind_ref, load_sem.at[3])
    for copy in loads:
        copy.start()

    def table_loads(i):
        return (
            pltpu.make_async_copy(high_in.at[i], high_ref.at[i], table_sem.at[0, i]),
            pltpu.make_async_copy(low_in.at[i], low_ref.at[i], table_sem.at[1, i]),
        )

    @pl.when(filtered)
    def _():
        for i in range(steps):
            for copy in table_loads(i):
                copy.start()

    load_wind.start()
    pl.semaphore_wait(barrier, sum(side.astype(jnp.int32) for side in has))

    def remote(source, target, send, recv, to):
        return pltpu.make_async_remote_copy(
            src_ref=source, dst_ref=target, send_sem=send, recv_sem=recv,
            device_id=there[to], device_id_type=MESH,
        )

    edge_level = (0, levels - 1)

    def wind_copy(to):
        return remote(
            wind_in.at[edge_level[to]], lev_wind.at[1 - to], wind_send.at[to], wind_recv.at[1 - to], to
        )

    def raw_copy(to, f, h):
        span = pl.ds(h * half, half)
        return remote(
            inputs[f].at[edge_level[to], span], lev_field.at[1 - to, f, span],
            raw_send.at[to, f, h], raw_recv.at[1 - to, f, h], to,
        )

    def spec_copy(to, i):
        return remote(
            spec.at[i, pl.ds(edge_level[to] * edge, edge)], spec_in.at[1 - to, i],
            spec_send.at[to, i], spec_recv.at[1 - to, i], to,
        )

    def lat_copy(to):
        return remote(lat_out.at[to], lat_in.at[1 - to], lat_send.at[to], lat_recv.at[1 - to], 2 + to)

    for to in range(2):
        for h in range(2):
            @pl.when(jnp.logical_and(has[to], raw[h]))
            def _():
                for f in range(3):
                    raw_copy(to, f, h).start()

        @pl.when(jnp.logical_and(has[to], jnp.logical_not(filtered)))
        def _():
            wind_copy(to).start()

    for side in range(2):
        for h in range(2):
            @pl.when(jnp.logical_not(jnp.logical_and(has[side], raw[h])))
            def _():
                for f in range(3):
                    lev_field[side, f, pl.ds(h * half, half), :] = jnp.zeros((half, NLON), jnp.float32)

        @pl.when(jnp.logical_not(has[side]))
        def _():
            lev_wind[side] = jnp.zeros(lev_wind.shape[1:], jnp.float32)

        @pl.when(jnp.logical_not(has[2 + side]))
        def _():
            lat_in[side] = jnp.zeros(lat_in.shape[1:], jnp.float32)

    row = lax.broadcasted_iota(jnp.int32, (lat_rows, 1), 0)
    for copy in loads:
        copy.wait()

    @pl.when(filtered)
    def _():
        cut = jnp.zeros((lat_rows, 1), jnp.int32)
        for j in range(lat_rows):
            cut = jnp.where(row == j, cut_ref[first_row + j], cut)

        for l in range(levels):
            for f in range(3):
                x = field_ref[f, l]
                first, second = x[:, :HALF], x[:, HALF:]
                at = pl.ds(l * edge + f * lat_rows, lat_rows)
                for p, folded in enumerate((first + second, first - second)):
                    high, low = split(folded)
                    xh[p, at, :] = high
                    xl[p, at, :] = low

        def forward(i, carry):
            parity, chunk = i // chunks, i % chunks
            for copy in table_loads(i):
                copy.wait()
            th, tl = high_ref[i], low_ref[i]
            part = dot(xh[parity], th) + dot(xl[parity], th) + dot(xh[parity], tl)
            lane = lax.broadcasted_iota(jnp.int32, (lat_rows, 2 * CHUNK), 1) % CHUNK
            mode = 2 * (chunk * CHUNK + lane) + parity
            weight = jnp.where(mode == 0, jnp.float32(1.0 / NLON), jnp.float32(2.0 / NLON))
            weight = jnp.where(mode <= cut, weight, 0.0)
            part = part * jnp.concatenate([weight] * (3 * levels), axis=0)
            spec[i] = part
            for to in range(2):
                @pl.when(has[to])
                def _():
                    spec_copy(to, i).start()
            high, low = split(part)
            sh[i, pl.ds(0, rows), :] = high
            sl[i, pl.ds(0, rows), :] = low
            return carry

        lax.fori_loop(0, steps, forward, 0)
        for to in range(2):
            @pl.when(has[to])
            def _():
                wind_copy(to).start()

        def backward(i, carry):
            parity, chunk = i // chunks, i % chunks
            for side in range(2):
                at = pl.ds(rows + slot_of[side] * edge, edge)

                @pl.when(has[side])
                def _():
                    spec_copy(1 - side, i).wait_recv()
                    high, low = split(spec_in[side, i])
                    sh[i, at, :] = high
                    sl[i, at, :] = low

                if slots == 2:
                    @pl.when(jnp.logical_not(has[side]))
                    def _():
                        sh[i, at, :] = jnp.zeros((edge, 2 * CHUNK), jnp.bfloat16)
                        sl[i, at, :] = jnp.zeros((edge, 2 * CHUNK), jnp.bfloat16)

            th, tl = high_ref[i], low_ref[i]
            part = dot(sh[i], th, True) + dot(sl[i], th, True) + dot(sh[i], tl, True)

            @pl.when(chunk == 0)
            def _():
                acc[parity] = part

            @pl.when(chunk > 0)
            def _():
                acc[parity] += part

            return carry

        lax.fori_loop(0, steps, backward, 0)
        keep = cut < HALF

        def value(at):
            even, odd = acc[0, at, :], acc[1, at, :]
            return jnp.concatenate([even + odd, even - odd], axis=1)

        for l in range(levels):
            for f in range(3):
                y = value(pl.ds(l * edge + f * lat_rows, lat_rows))
                field_ref[f, l] = jnp.where(keep, y, field_ref[f, l])
        for side in range(2):
            for h in range(2):
                @pl.when(jnp.logical_and(has[side], raw[h]))
                def _():
                    for f in range(3):
                        raw_copy(1 - side, f, h).wait_recv()

            @pl.when(has[side])
            def _():
                for f in range(3):
                    y = value(pl.ds(rows + slot_of[side] * edge + f * lat_rows, lat_rows))
                    lev_field[side, f] = jnp.where(keep, y, lev_field[side, f])

    for to, at in ((0, 0), (1, lat_rows - 1)):
        for f in range(3):
            for l in range(levels):
                lat_out[to, f * levels + l : f * levels + l + 1, :] = field_ref[f, l, at : at + 1, :]

        @pl.when(has[2 + to])
        def _():
            lat_copy(to).start()

    load_wind.wait()
    factors = factor_ref[pl.ds(pl.multiple_of(first_row, lat_rows), lat_rows), :]
    low_face = jnp.where(row > 0, factors[:, 0:1], 0.0)
    high_face = jnp.where(row < lat_rows - 1, factors[:, 1:2], 0.0)
    zonal_factor = factors[:, 2:3]

    def inner(l, carry):
        below, above = jnp.maximum(l - 1, 0), jnp.minimum(l + 1, levels - 1)
        zonal = field_ref[0, l]
        merid = field_ref[1, l]
        wind_here = wind_ref[l]
        east_wind = (zonal + east_of(zonal)) * zonal_factor
        merid_pair = merid + jnp.roll(merid, 1, axis=0)
        low_wind = jnp.where(l > 0, jnp.float32(QUARTER), 0.0) * (wind_ref[below] + wind_here)
        high_wind = jnp.where(l < levels - 1, jnp.float32(QUARTER), 0.0) * (wind_here + wind_ref[above])
        for f in range(3):
            x = field_ref[f, l]
            flux_x = east_wind * (x + east_of(x))
            flux_y = merid_pair * (x + jnp.roll(x, 1, axis=0))
            div_y = high_face * jnp.roll(flux_y, -1, axis=0) - low_face * flux_y
            div_z = high_wind * (x + field_ref[f, above]) - low_wind * (field_ref[f, below] + x)
            outs[f][l] = x - (flux_x - west_of(flux_x)) - div_y - div_z
        return carry

    lax.fori_loop(0, levels, inner, 0)

    for side in range(2):
        @pl.when(has[2 + side])
        def _():
            lat_copy(1 - side).wait_recv()
    for side, at, factor in ((0, 0, factors[0:1, 0:1]), (1, lat_rows - 1, -factors[lat_rows - 1 :, 1:2])):
        for l in range(levels):
            own = pl.ds(at, 1)
            pair = factor * (lat_in[side, levels + l : levels + l + 1, :] + field_ref[1, l, own, :])
            for f in range(3):
                halo = lat_in[side, f * levels + l : f * levels + l + 1, :]
                outs[f][l, own, :] += pair * (halo + field_ref[f, l, own, :])

    for side in range(2):
        @pl.when(has[side])
        def _():
            wind_copy(1 - side).wait_recv()

        for h in range(2):
            @pl.when(jnp.logical_and(jnp.logical_and(has[side], raw[h]), jnp.logical_not(filtered)))
            def _():
                for f in range(3):
                    raw_copy(1 - side, f, h).wait_recv()
    for side, l, sign in ((0, 0, QUARTER), (1, levels - 1, -QUARTER)):
        pair = sign * (lev_wind[side] + wind_ref[l])
        for f in range(3):
            outs[f][l] += pair * (lev_field[side, f] + field_ref[f, l])
    for to in range(2):
        @pl.when(has[to])
        def _():
            wind_copy(to).wait_send()

        @pl.when(jnp.logical_and(has[to], filtered))
        def _():
            for i in range(steps):
                spec_copy(to, i).wait_send()

        for h in range(2):
            @pl.when(jnp.logical_and(has[to], raw[h]))
            def _():
                for f in range(3):
                    raw_copy(to, f, h).wait_send()

        @pl.when(has[2 + to])
        def _():
            lat_copy(to).wait_send()


def solution(mesh):
    lat_count, lev_count = mesh.shape["lat"], mesh.shape["lev"]

    def on_device(zonal_wind, merid_wind, tracer, vertical_wind, cutoff):
        levels, lat_rows, _ = zonal_wind.shape
        total_rows = lat_rows * lat_count
        cap = total_rows * 40 // 256
        high, low = half_tables()
        steps = high.shape[0]
        edge = 3 * lat_rows
        rows = levels * edge
        wide = rows + edge * (1 if lev_count == 2 else 2)
        vmem = pl.BlockSpec(memory_space=pltpu.VMEM)
        smem = pl.BlockSpec(memory_space=pltpu.SMEM)
        hbm = pl.BlockSpec(memory_space=pl.ANY)
        one = jax.ShapeDtypeStruct(zonal_wind.shape, jnp.float32)
        dma = pltpu.SemaphoreType.DMA
        return pl.pallas_call(
            lambda *refs: kernel(lat_count, lev_count, cap, *refs),
            out_shape=(one, one, one),
            in_specs=[hbm] * 4 + [smem, vmem, hbm, hbm],
            out_specs=(vmem,) * 3,
            scratch_shapes=[
                pltpu.VMEM((3, levels, lat_rows, NLON), jnp.float32),
                pltpu.VMEM((levels, lat_rows, NLON), jnp.float32),
                pltpu.VMEM(high.shape, jnp.bfloat16),
                pltpu.VMEM(low.shape, jnp.bfloat16),
                pltpu.VMEM((2, rows, HALF), jnp.bfloat16),
                pltpu.VMEM((2, rows, HALF), jnp.bfloat16),
                pltpu.VMEM((steps, rows, 2 * CHUNK), jnp.float32),
                pltpu.VMEM((2, steps, edge, 2 * CHUNK), jnp.float32),
                pltpu.VMEM((steps, wide, 2 * CHUNK), jnp.bfloat16),
                pltpu.VMEM((steps, wide, 2 * CHUNK), jnp.bfloat16),
                pltpu.VMEM((2, wide, HALF), jnp.float32),
                pltpu.VMEM((2, 3, lat_rows, NLON), jnp.float32),
                pltpu.VMEM((2, lat_rows, NLON), jnp.float32),
                pltpu.VMEM((2, 3 * levels, NLON), jnp.float32),
                pltpu.VMEM((2, 3 * levels, NLON), jnp.float32),
                dma((4,)), dma((2, steps)), dma((2,)), dma((2,)), dma((2, 3, 2)), dma((2, 3, 2)),
                dma((2, steps)), dma((2, steps)), dma((2,)), dma((2,)),
            ],
            compiler_params=pltpu.CompilerParams(
                collective_id=0, has_side_effects=True, vmem_limit_bytes=58 * 1024 * 1024
            ),
        )(
            zonal_wind, merid_wind, tracer, vertical_wind, cutoff,
            jnp.asarray(latitude_factors(total_rows)), jnp.asarray(high), jnp.asarray(low),
        )

    spec = P("lev", "lat", None)
    return jax.shard_map(
        on_device, mesh=mesh, in_specs=(spec,) * 4 + (P(),), out_specs=(spec,) * 3, check_vma=False
    )
```

```python
import math

import jax
import jax.numpy as jnp
import ml_dtypes
import numpy as np
from jax import lax
from jax.experimental import pallas as pl
from jax.experimental.pallas import tpu as pltpu
from jax.sharding import PartitionSpec as P

NLON = 2880
KMAX = 720
HALF = NLON // 2
CHUNK = 128
MESH = pl.DeviceIdType.MESH
QUARTER = 0.025


def half_tables():
    modes = KMAX // 2
    chunks = -(-modes // CHUNK)
    tables = np.zeros((2, chunks, HALF, 2 * CHUNK), np.float32)
    points = np.arange(HALF, dtype=np.int64)
    for parity in range(2):
        for chunk in range(chunks):
            ids = np.arange(chunk * CHUNK, min((chunk + 1) * CHUNK, modes), dtype=np.int64)
            angles = (points[:, None] * (2 * ids + parity)[None, :] % NLON) * (2.0 * math.pi / NLON)
            tables[parity, chunk, :, : len(ids)] = np.cos(angles)
            tables[parity, chunk, :, CHUNK : CHUNK + len(ids)] = np.sin(angles)
    tables = tables.reshape(2 * chunks, HALF, 2 * CHUNK)
    high = tables.astype(ml_dtypes.bfloat16)
    low = (tables - high.astype(np.float32)).astype(ml_dtypes.bfloat16)
    return high, low


def split(x):
    high = x.astype(jnp.bfloat16)
    return high, (x - high.astype(jnp.float32)).astype(jnp.bfloat16)


def dot(a, b, transposed=False):
    dims = (((1,), (1 if transposed else 0,)), ((), ()))
    return lax.dot_general(a, b, dims, preferred_element_type=jnp.float32)


def latitude_factors(total_rows):
    ids = np.arange(total_rows + 1, dtype=np.float64)
    face = np.sin(ids * (math.pi / total_rows))
    center = np.sin((ids[:-1] + 0.5) * (math.pi / total_rows))
    return np.stack(
        [QUARTER * face[:-1] / center, QUARTER * face[1:] / center, QUARTER / center], axis=1
    ).astype(np.float32)


def east_of(x):
    return jnp.concatenate([x[:, 1:], x[:, :1]], axis=1)


def west_of(x):
    return jnp.concatenate([x[:, -1:], x[:, :-1]], axis=1)


def kernel(
    lat_count, lev_count, cap, zonal_in, merid_in, tracer_in, wind_in, cut_ref, factor_ref, high_in, low_in,
    out0, out1, out2,
    field_ref, wind_ref, high_ref, low_ref, xh, xl, spec, spec_in, sh, sl, acc,
    lev_field, lev_wind, lat_out, lat_in,
    load_sem, table_sem, wind_send, wind_recv, raw_send, raw_recv, spec_send, spec_recv, lat_send, lat_recv,
):
    lat, lev = lax.axis_index("lat"), lax.axis_index("lev")
    inputs = (zonal_in, merid_in, tracer_in)
    outs = (out0, out1, out2)
    levels, lat_rows = wind_ref.shape[0], wind_ref.shape[1]
    steps = high_ref.shape[0]
    chunks = steps // 2
    edge = 3 * lat_rows
    rows = levels * edge
    half = lat_rows // 2
    total_rows = lat_count * lat_rows
    has = (lev > 0, lev < lev_count - 1, lat > 0, lat < lat_count - 1)
    there = ((lat, lev - 1), (lat, lev + 1), (lat - 1, lev), (lat + 1, lev))
    slots = 1 if lev_count == 2 else 2
    slot_of = (0, slots - 1)
    first_row = lat * lat_rows

    def spans(start, count):
        some = jnp.logical_or(start < cap, start + count > total_rows - cap)
        inside = jnp.logical_and(start + count > cap, start < total_rows - cap)
        return some, inside

    filtered, _ = spans(first_row, lat_rows)
    raw = tuple(spans(first_row + h * half, half)[1] for h in range(2))

    barrier = pltpu.get_barrier_semaphore()
    for side in range(4):
        @pl.when(has[side])
        def _():
            pl.semaphore_signal(barrier, inc=1, device_id=there[side], device_id_type=MESH)

    loads = [pltpu.make_async_copy(inputs[f], field_ref.at[f], load_sem.at[f]) for f in range(3)]
    load_wind = pltpu.make_async_copy(wind_in, wind_ref, load_sem.at[3])
    for copy in loads:
        copy.start()

    def table_loads(i):
        return (
            pltpu.make_async_copy(high_in.at[i], high_ref.at[i], table_sem.at[0, i]),
            pltpu.make_async_copy(low_in.at[i], low_ref.at[i], table_sem.at[1, i]),
        )

    @pl.when(filtered)
    def _():
        for i in range(steps):
            for copy in table_loads(i):
                copy.start()

    load_wind.start()
    pl.semaphore_wait(barrier, sum(side.astype(jnp.int32) for side in has))

    def remote(source, target, send, recv, to):
        return pltpu.make_async_remote_copy(
            src_ref=source, dst_ref=target, send_sem=send, recv_sem=recv,
            device_id=there[to], device_id_type=MESH,
        )

    edge_level = (0, levels - 1)

    def wind_copy(to):
        return remote(
            wind_in.at[edge_level[to]], lev_wind.at[1 - to], wind_send.at[to], wind_recv.at[1 - to], to
        )

    def raw_copy(to, f, h):
        span = pl.ds(h * half, half)
        return remote(
            inputs[f].at[edge_level[to], span], lev_field.at[1 - to, f, span],
            raw_send.at[to, f, h], raw_recv.at[1 - to, f, h], to,
        )

    def spec_copy(to, i):
        return remote(
            spec.at[i, pl.ds(edge_level[to] * edge, edge)], spec_in.at[1 - to, i],
            spec_send.at[to, i], spec_recv.at[1 - to, i], to,
        )

    def lat_copy(to):
        return remote(lat_out.at[to], lat_in.at[1 - to], lat_send.at[to], lat_recv.at[1 - to], 2 + to)

    for to in range(2):
        for h in range(2):
            @pl.when(jnp.logical_and(has[to], raw[h]))
            def _():
                for f in range(3):
                    raw_copy(to, f, h).start()

        @pl.when(jnp.logical_and(has[to], jnp.logical_not(filtered)))
        def _():
            wind_copy(to).start()

    for side in range(2):
        for h in range(2):
            @pl.when(jnp.logical_not(jnp.logical_and(has[side], raw[h])))
            def _():
                for f in range(3):
                    lev_field[side, f, pl.ds(h * half, half), :] = jnp.zeros((half, NLON), jnp.float32)

        @pl.when(jnp.logical_not(has[side]))
        def _():
            lev_wind[side] = jnp.zeros(lev_wind.shape[1:], jnp.float32)

        @pl.when(jnp.logical_not(has[2 + side]))
        def _():
            lat_in[side] = jnp.zeros(lat_in.shape[1:], jnp.float32)

    row = lax.broadcasted_iota(jnp.int32, (lat_rows, 1), 0)
    for copy in loads:
        copy.wait()

    def own_cut():
        cut = jnp.zeros((lat_rows, 1), jnp.int32)
        for j in range(lat_rows):
            cut = jnp.where(row == j, cut_ref[first_row + j], cut)
        return cut

    def value(at):
        even, odd = acc[0, at, :], acc[1, at, :]
        return jnp.concatenate([even + odd, even - odd], axis=1)

    @pl.when(filtered)
    def _():
        cut = own_cut()

        for l in range(levels):
            for f in range(3):
                x = field_ref[f, l]
                first, second = x[:, :HALF], x[:, HALF:]
                at = pl.ds(l * edge + f * lat_rows, lat_rows)
                for p, folded in enumerate((first + second, first - second)):
                    high, low = split(folded)
                    xh[p, at, :] = high
                    xl[p, at, :] = low

        def forward(i, carry):
            parity, chunk = i // chunks, i % chunks
            for copy in table_loads(i):
                copy.wait()
            th, tl = high_ref[i], low_ref[i]
            part = dot(xh[parity], th) + dot(xl[parity], th) + dot(xh[parity], tl)
            lane = lax.broadcasted_iota(jnp.int32, (lat_rows, 2 * CHUNK), 1) % CHUNK
            mode = 2 * (chunk * CHUNK + lane) + parity
            weight = jnp.where(mode == 0, jnp.float32(1.0 / NLON), jnp.float32(2.0 / NLON))
            weight = jnp.where(mode <= cut, weight, 0.0)
            part = part * jnp.concatenate([weight] * (3 * levels), axis=0)
            spec[i] = part
            for to in range(2):
                @pl.when(has[to])
                def _():
                    spec_copy(to, i).start()
            high, low = split(part)
            sh[i, pl.ds(0, rows), :] = high
            sl[i, pl.ds(0, rows), :] = low
            return carry

        lax.fori_loop(0, steps, forward, 0)
        for to in range(2):
            @pl.when(has[to])
            def _():
                wind_copy(to).start()

        def backward(i, carry):
            parity, chunk = i // chunks, i % chunks
            for side in range(2):
                at = pl.ds(rows + slot_of[side] * edge, edge)

                @pl.when(has[side])
                def _():
                    spec_copy(1 - side, i).wait_recv()
                    high, low = split(spec_in[side, i])
                    sh[i, at, :] = high
                    sl[i, at, :] = low

                if slots == 2:
                    @pl.when(jnp.logical_not(has[side]))
                    def _():
                        sh[i, at, :] = jnp.zeros((edge, 2 * CHUNK), jnp.bfloat16)
                        sl[i, at, :] = jnp.zeros((edge, 2 * CHUNK), jnp.bfloat16)

            th, tl = high_ref[i], low_ref[i]
            part = dot(sh[i], th, True) + dot(sl[i], th, True) + dot(sh[i], tl, True)

            @pl.when(chunk == 0)
            def _():
                acc[parity] = part

            @pl.when(chunk > 0)
            def _():
                acc[parity] += part

            return carry

        lax.fori_loop(0, steps, backward, 0)
        keep = cut < HALF

        for l in range(levels):
            for f in range(3):
                y = value(pl.ds(l * edge + f * lat_rows, lat_rows))
                field_ref[f, l] = jnp.where(keep, y, field_ref[f, l])

    for to, at in ((0, 0), (1, lat_rows - 1)):
        for f in range(3):
            for l in range(levels):
                lat_out[to, f * levels + l : f * levels + l + 1, :] = field_ref[f, l, at : at + 1, :]

        @pl.when(has[2 + to])
        def _():
            lat_copy(to).start()

    load_wind.wait()
    factors = factor_ref[pl.ds(pl.multiple_of(first_row, lat_rows), lat_rows), :]
    low_face = jnp.where(row > 0, factors[:, 0:1], 0.0)
    high_face = jnp.where(row < lat_rows - 1, factors[:, 1:2], 0.0)
    zonal_factor = factors[:, 2:3]

    def inner(l, carry):
        below, above = jnp.maximum(l - 1, 0), jnp.minimum(l + 1, levels - 1)
        zonal = field_ref[0, l]
        merid = field_ref[1, l]
        wind_here = wind_ref[l]
        east_wind = (zonal + east_of(zonal)) * zonal_factor
        merid_pair = merid + jnp.roll(merid, 1, axis=0)
        low_wind = jnp.where(l > 0, jnp.float32(QUARTER), 0.0) * (wind_ref[below] + wind_here)
        high_wind = jnp.where(l < levels - 1, jnp.float32(QUARTER), 0.0) * (wind_here + wind_ref[above])
        for f in range(3):
            x = field_ref[f, l]
            flux_x = east_wind * (x + east_of(x))
            flux_y = merid_pair * (x + jnp.roll(x, 1, axis=0))
            div_y = high_face * jnp.roll(flux_y, -1, axis=0) - low_face * flux_y
            div_z = high_wind * (x + field_ref[f, above]) - low_wind * (field_ref[f, below] + x)
            outs[f][l] = x - (flux_x - west_of(flux_x)) - div_y - div_z
        return carry

    lax.fori_loop(0, levels, inner, 0)

    for side in range(2):
        @pl.when(has[2 + side])
        def _():
            lat_copy(1 - side).wait_recv()
    for side, at, factor in ((0, 0, factors[0:1, 0:1]), (1, lat_rows - 1, -factors[lat_rows - 1 :, 1:2])):
        for l in range(levels):
            own = pl.ds(at, 1)
            pair = factor * (lat_in[side, levels + l : levels + l + 1, :] + field_ref[1, l, own, :])
            for f in range(3):
                halo = lat_in[side, f * levels + l : f * levels + l + 1, :]
                outs[f][l, own, :] += pair * (halo + field_ref[f, l, own, :])

    for side in range(2):
        @pl.when(has[side])
        def _():
            wind_copy(1 - side).wait_recv()

        for h in range(2):
            @pl.when(jnp.logical_and(has[side], raw[h]))
            def _():
                for f in range(3):
                    raw_copy(1 - side, f, h).wait_recv()

        @pl.when(jnp.logical_and(has[side], filtered))
        def _():
            keep = own_cut() < HALF
            for f in range(3):
                y = value(pl.ds(rows + slot_of[side] * edge + f * lat_rows, lat_rows))
                lev_field[side, f] = jnp.where(keep, y, lev_field[side, f])
    for side, l, sign in ((0, 0, QUARTER), (1, levels - 1, -QUARTER)):
        pair = sign * (lev_wind[side] + wind_ref[l])
        for f in range(3):
            outs[f][l] += pair * (lev_field[side, f] + field_ref[f, l])
    for to in range(2):
        @pl.when(has[to])
        def _():
            wind_copy(to).wait_send()

        @pl.when(jnp.logical_and(has[to], filtered))
        def _():
            for i in range(steps):
                spec_copy(to, i).wait_send()

        for h in range(2):
            @pl.when(jnp.logical_and(has[to], raw[h]))
            def _():
                for f in range(3):
                    raw_copy(to, f, h).wait_send()

        @pl.when(has[2 + to])
        def _():
            lat_copy(to).wait_send()


def store_kernel(*refs):
    for f in range(3):
        refs[3 + f][...] = refs[f][...]


def stored(fields):
    levels, lat_rows, _ = fields[0].shape
    block = pl.BlockSpec((1, lat_rows, NLON), lambda l: (l, 0, 0))
    one = jax.ShapeDtypeStruct(fields[0].shape, jnp.float32)
    return pl.pallas_call(
        store_kernel, grid=(levels,), out_shape=(one,) * 3, in_specs=[block] * 3, out_specs=(block,) * 3,
        compiler_params=pltpu.CompilerParams(vmem_limit_bytes=58 * 1024 * 1024),
    )(*fields)


def solution(mesh):
    lat_count, lev_count = mesh.shape["lat"], mesh.shape["lev"]

    def on_device(zonal_wind, merid_wind, tracer, vertical_wind, cutoff):
        levels, lat_rows, _ = zonal_wind.shape
        total_rows = lat_rows * lat_count
        cap = total_rows * 40 // 256
        high, low = half_tables()
        steps = high.shape[0]
        edge = 3 * lat_rows
        rows = levels * edge
        wide = rows + edge * (1 if lev_count == 2 else 2)
        vmem = pl.BlockSpec(memory_space=pltpu.VMEM)
        smem = pl.BlockSpec(memory_space=pltpu.SMEM)
        hbm = pl.BlockSpec(memory_space=pl.ANY)
        one = jax.ShapeDtypeStruct(zonal_wind.shape, jnp.float32)
        dma = pltpu.SemaphoreType.DMA
        fields = pl.pallas_call(
            lambda *refs: kernel(lat_count, lev_count, cap, *refs),
            out_shape=(one, one, one),
            in_specs=[hbm] * 4 + [smem, vmem, hbm, hbm],
            out_specs=(vmem,) * 3,
            scratch_shapes=[
                pltpu.VMEM((3, levels, lat_rows, NLON), jnp.float32),
                pltpu.VMEM((levels, lat_rows, NLON), jnp.float32),
                pltpu.VMEM(high.shape, jnp.bfloat16),
                pltpu.VMEM(low.shape, jnp.bfloat16),
                pltpu.VMEM((2, rows, HALF), jnp.bfloat16),
                pltpu.VMEM((2, rows, HALF), jnp.bfloat16),
                pltpu.VMEM((steps, rows, 2 * CHUNK), jnp.float32),
                pltpu.VMEM((2, steps, edge, 2 * CHUNK), jnp.float32),
                pltpu.VMEM((steps, wide, 2 * CHUNK), jnp.bfloat16),
                pltpu.VMEM((steps, wide, 2 * CHUNK), jnp.bfloat16),
                pltpu.VMEM((2, wide, HALF), jnp.float32),
                pltpu.VMEM((2, 3, lat_rows, NLON), jnp.float32),
                pltpu.VMEM((2, lat_rows, NLON), jnp.float32),
                pltpu.VMEM((2, 3 * levels, NLON), jnp.float32),
                pltpu.VMEM((2, 3 * levels, NLON), jnp.float32),
                dma((4,)), dma((2, steps)), dma((2,)), dma((2,)), dma((2, 3, 2)), dma((2, 3, 2)),
                dma((2, steps)), dma((2, steps)), dma((2,)), dma((2,)),
            ],
            compiler_params=pltpu.CompilerParams(
                collective_id=0, has_side_effects=True, vmem_limit_bytes=58 * 1024 * 1024
            ),
        )(
            zonal_wind, merid_wind, tracer, vertical_wind, cutoff,
            jnp.asarray(latitude_factors(total_rows)), jnp.asarray(high), jnp.asarray(low),
        )
        return stored(fields)

    spec = P("lev", "lat", None)
    return jax.shard_map(
        on_device, mesh=mesh, in_specs=(spec,) * 4 + (P(),), out_specs=(spec,) * 3, check_vma=False
    )
```

```python
import math

import jax
import jax.numpy as jnp
import ml_dtypes
import numpy as np
from jax import lax
from jax.experimental import pallas as pl
from jax.experimental.pallas import tpu as pltpu
from jax.sharding import PartitionSpec as P

NLON = 2880
KMAX = 720
HALF = NLON // 2
CHUNK = 128
MESH = pl.DeviceIdType.MESH
QUARTER = 0.025


def half_tables():
    modes = KMAX // 2
    chunks = -(-modes // CHUNK)
    tables = np.zeros((2, chunks, HALF, 2 * CHUNK), np.float32)
    points = np.arange(HALF, dtype=np.int64)
    for parity in range(2):
        for chunk in range(chunks):
            ids = np.arange(chunk * CHUNK, min((chunk + 1) * CHUNK, modes), dtype=np.int64)
            angles = (points[:, None] * (2 * ids + parity)[None, :] % NLON) * (2.0 * math.pi / NLON)
            tables[parity, chunk, :, : len(ids)] = np.cos(angles)
            tables[parity, chunk, :, CHUNK : CHUNK + len(ids)] = np.sin(angles)
    tables = tables.reshape(2 * chunks, HALF, 2 * CHUNK)
    high = tables.astype(ml_dtypes.bfloat16)
    low = (tables - high.astype(np.float32)).astype(ml_dtypes.bfloat16)
    return high, low


def split(x):
    high = x.astype(jnp.bfloat16)
    return high, (x - high.astype(jnp.float32)).astype(jnp.bfloat16)


def dot(a, b, transposed=False):
    dims = (((1,), (1 if transposed else 0,)), ((), ()))
    return lax.dot_general(a, b, dims, preferred_element_type=jnp.float32)


def latitude_factors(total_rows):
    ids = np.arange(total_rows + 1, dtype=np.float64)
    face = np.sin(ids * (math.pi / total_rows))
    center = np.sin((ids[:-1] + 0.5) * (math.pi / total_rows))
    return np.stack(
        [QUARTER * face[:-1] / center, QUARTER * face[1:] / center, QUARTER / center], axis=1
    ).astype(np.float32)


def east_of(x):
    return jnp.concatenate([x[:, 1:], x[:, :1]], axis=1)


def west_of(x):
    return jnp.concatenate([x[:, -1:], x[:, :-1]], axis=1)


def kernel(
    lat_count, lev_count, cap, zonal_in, merid_in, tracer_in, wind_in, cut_ref, factor_ref, high_in, low_in,
    out0, out1, out2,
    field_ref, wind_ref, high_ref, low_ref, xh, xl, spec, spec_in, sh, sl, acc,
    lev_field, lev_wind, lat_out, lat_in, out_ref,
    load_sem, out_sem, table_sem, wind_send, wind_recv, raw_send, raw_recv, spec_send, spec_recv, lat_send, lat_recv,
):
    lat, lev = lax.axis_index("lat"), lax.axis_index("lev")
    inputs = (zonal_in, merid_in, tracer_in)
    results = (out0, out1, out2)
    outs = (out_ref.at[0], out_ref.at[1], out_ref.at[2])
    levels, lat_rows = wind_ref.shape[0], wind_ref.shape[1]
    steps = high_ref.shape[0]
    chunks = steps // 2
    edge = 3 * lat_rows
    rows = levels * edge
    half = lat_rows // 2
    total_rows = lat_count * lat_rows
    has = (lev > 0, lev < lev_count - 1, lat > 0, lat < lat_count - 1)
    there = ((lat, lev - 1), (lat, lev + 1), (lat - 1, lev), (lat + 1, lev))
    slots = 1 if lev_count == 2 else 2
    slot_of = (0, slots - 1)
    first_row = lat * lat_rows

    def spans(start, count):
        some = jnp.logical_or(start < cap, start + count > total_rows - cap)
        inside = jnp.logical_and(start + count > cap, start < total_rows - cap)
        return some, inside

    filtered, _ = spans(first_row, lat_rows)
    mixed = jnp.logical_and(filtered, spans(first_row, lat_rows)[1])
    pure = jnp.logical_and(filtered, jnp.logical_not(mixed))
    early = tuple(jnp.logical_not(spans(first_row + h * half, half)[0]) for h in range(2))
    late = tuple(jnp.logical_and(mixed, jnp.logical_not(early[h])) for h in range(2))

    def result_copy(f, l):
        return pltpu.make_async_copy(out_ref.at[f, l], results[f].at[l], out_sem.at[f, l])

    barrier = pltpu.get_barrier_semaphore()
    for side in range(4):
        @pl.when(has[side])
        def _():
            pl.semaphore_signal(barrier, inc=1, device_id=there[side], device_id_type=MESH)

    loads = [pltpu.make_async_copy(inputs[f], field_ref.at[f], load_sem.at[f]) for f in range(3)]
    load_wind = pltpu.make_async_copy(wind_in, wind_ref, load_sem.at[3])
    for copy in loads:
        copy.start()

    def table_loads(i):
        return (
            pltpu.make_async_copy(high_in.at[i], high_ref.at[i], table_sem.at[0, i]),
            pltpu.make_async_copy(low_in.at[i], low_ref.at[i], table_sem.at[1, i]),
        )

    @pl.when(filtered)
    def _():
        for i in range(steps):
            for copy in table_loads(i):
                copy.start()

    load_wind.start()
    pl.semaphore_wait(barrier, sum(side.astype(jnp.int32) for side in has))

    def remote(source, target, send, recv, to):
        return pltpu.make_async_remote_copy(
            src_ref=source, dst_ref=target, send_sem=send, recv_sem=recv,
            device_id=there[to], device_id_type=MESH,
        )

    edge_level = (0, levels - 1)

    def wind_copy(to):
        return remote(
            wind_in.at[edge_level[to]], lev_wind.at[1 - to], wind_send.at[to], wind_recv.at[1 - to], to
        )

    def raw_copy(to, f, h, source=inputs):
        span = pl.ds(h * half, half)
        return remote(
            source[f].at[edge_level[to], span], lev_field.at[1 - to, f, span],
            raw_send.at[to, f, h], raw_recv.at[1 - to, f, h], to,
        )

    def spec_copy(to, i):
        return remote(
            spec.at[i, pl.ds(edge_level[to] * edge, edge)], spec_in.at[1 - to, i],
            spec_send.at[to, i], spec_recv.at[1 - to, i], to,
        )

    def lat_copy(to):
        return remote(lat_out.at[to], lat_in.at[1 - to], lat_send.at[to], lat_recv.at[1 - to], 2 + to)

    for to in range(2):
        for h in range(2):
            @pl.when(jnp.logical_and(has[to], early[h]))
            def _():
                for f in range(3):
                    raw_copy(to, f, h).start()

        @pl.when(jnp.logical_and(has[to], jnp.logical_not(pure)))
        def _():
            wind_copy(to).start()

    for side in range(2):
        @pl.when(jnp.logical_or(jnp.logical_not(has[side]), pure))
        def _():
            lev_field[side] = jnp.zeros(lev_field.shape[1:], jnp.float32)

        @pl.when(jnp.logical_not(has[side]))
        def _():
            lev_wind[side] = jnp.zeros(lev_wind.shape[1:], jnp.float32)

        @pl.when(jnp.logical_not(has[2 + side]))
        def _():
            lat_in[side] = jnp.zeros(lat_in.shape[1:], jnp.float32)

    row = lax.broadcasted_iota(jnp.int32, (lat_rows, 1), 0)
    for copy in loads:
        copy.wait()

    def own_cut():
        cut = jnp.zeros((lat_rows, 1), jnp.int32)
        for j in range(lat_rows):
            cut = jnp.where(row == j, cut_ref[first_row + j], cut)
        return cut

    def value(at):
        even, odd = acc[0, at, :], acc[1, at, :]
        return jnp.concatenate([even + odd, even - odd], axis=1)

    @pl.when(filtered)
    def _():
        cut = own_cut()

        for l in range(levels):
            for f in range(3):
                x = field_ref[f, l]
                first, second = x[:, :HALF], x[:, HALF:]
                at = pl.ds(l * edge + f * lat_rows, lat_rows)
                for p, folded in enumerate((first + second, first - second)):
                    high, low = split(folded)
                    xh[p, at, :] = high
                    xl[p, at, :] = low

        def forward(i, carry):
            parity, chunk = i // chunks, i % chunks
            for copy in table_loads(i):
                copy.wait()
            th, tl = high_ref[i], low_ref[i]
            part = dot(xh[parity], th) + dot(xl[parity], th) + dot(xh[parity], tl)
            lane = lax.broadcasted_iota(jnp.int32, (lat_rows, 2 * CHUNK), 1) % CHUNK
            mode = 2 * (chunk * CHUNK + lane) + parity
            weight = jnp.where(mode == 0, jnp.float32(1.0 / NLON), jnp.float32(2.0 / NLON))
            weight = jnp.where(mode <= cut, weight, 0.0)
            part = part * jnp.concatenate([weight] * (3 * levels), axis=0)
            spec[i] = part
            for to in range(2):
                @pl.when(jnp.logical_and(has[to], pure))
                def _():
                    spec_copy(to, i).start()
            high, low = split(part)
            sh[i, pl.ds(0, rows), :] = high
            sl[i, pl.ds(0, rows), :] = low
            return carry

        lax.fori_loop(0, steps, forward, 0)
        for to in range(2):
            @pl.when(jnp.logical_and(has[to], pure))
            def _():
                wind_copy(to).start()

        def backward(i, carry):
            parity, chunk = i // chunks, i % chunks
            for side in range(2):
                at = pl.ds(rows + slot_of[side] * edge, edge)

                @pl.when(jnp.logical_and(has[side], pure))
                def _():
                    spec_copy(1 - side, i).wait_recv()
                    high, low = split(spec_in[side, i])
                    sh[i, at, :] = high
                    sl[i, at, :] = low

                empty = jnp.logical_not(jnp.logical_and(has[side], pure)) if slots == 2 else mixed

                @pl.when(empty)
                def _():
                    sh[i, at, :] = jnp.zeros((edge, 2 * CHUNK), jnp.bfloat16)
                    sl[i, at, :] = jnp.zeros((edge, 2 * CHUNK), jnp.bfloat16)

            th, tl = high_ref[i], low_ref[i]
            part = dot(sh[i], th, True) + dot(sl[i], th, True) + dot(sh[i], tl, True)

            @pl.when(chunk == 0)
            def _():
                acc[parity] = part

            @pl.when(chunk > 0)
            def _():
                acc[parity] += part

            return carry

        lax.fori_loop(0, steps, backward, 0)
        keep = cut < HALF

        for l in range(levels):
            for f in range(3):
                y = value(pl.ds(l * edge + f * lat_rows, lat_rows))
                field_ref[f, l] = jnp.where(keep, y, field_ref[f, l])

    for to in range(2):
        for h in range(2):
            @pl.when(jnp.logical_and(has[to], late[h]))
            def _():
                for f in range(3):
                    raw_copy(to, f, h, (field_ref.at[0], field_ref.at[1], field_ref.at[2])).start()

    for to, at in ((0, 0), (1, lat_rows - 1)):
        for f in range(3):
            for l in range(levels):
                lat_out[to, f * levels + l : f * levels + l + 1, :] = field_ref[f, l, at : at + 1, :]

        @pl.when(has[2 + to])
        def _():
            lat_copy(to).start()

    load_wind.wait()
    factors = factor_ref[pl.ds(pl.multiple_of(first_row, lat_rows), lat_rows), :]
    low_face = jnp.where(row > 0, factors[:, 0:1], 0.0)
    high_face = jnp.where(row < lat_rows - 1, factors[:, 1:2], 0.0)
    zonal_factor = factors[:, 2:3]

    def inner(l, carry):
        below, above = jnp.maximum(l - 1, 0), jnp.minimum(l + 1, levels - 1)
        zonal = field_ref[0, l]
        merid = field_ref[1, l]
        wind_here = wind_ref[l]
        east_wind = (zonal + east_of(zonal)) * zonal_factor
        merid_pair = merid + jnp.roll(merid, 1, axis=0)
        low_wind = jnp.where(l > 0, jnp.float32(QUARTER), 0.0) * (wind_ref[below] + wind_here)
        high_wind = jnp.where(l < levels - 1, jnp.float32(QUARTER), 0.0) * (wind_here + wind_ref[above])
        for f in range(3):
            x = field_ref[f, l]
            flux_x = east_wind * (x + east_of(x))
            flux_y = merid_pair * (x + jnp.roll(x, 1, axis=0))
            div_y = high_face * jnp.roll(flux_y, -1, axis=0) - low_face * flux_y
            div_z = high_wind * (x + field_ref[f, above]) - low_wind * (field_ref[f, below] + x)
            outs[f][l] = x - (flux_x - west_of(flux_x)) - div_y - div_z
        return carry

    lax.fori_loop(0, levels, inner, 0)

    for side in range(2):
        @pl.when(has[2 + side])
        def _():
            lat_copy(1 - side).wait_recv()
    for side, at, factor in ((0, 0, factors[0:1, 0:1]), (1, lat_rows - 1, -factors[lat_rows - 1 :, 1:2])):
        for l in range(levels):
            own = pl.ds(at, 1)
            pair = factor * (lat_in[side, levels + l : levels + l + 1, :] + field_ref[1, l, own, :])
            for f in range(3):
                halo = lat_in[side, f * levels + l : f * levels + l + 1, :]
                outs[f][l, own, :] += pair * (halo + field_ref[f, l, own, :])
    for l in range(1, levels - 1):
        for f in range(3):
            result_copy(f, l).start()

    for side in range(2):
        @pl.when(has[side])
        def _():
            wind_copy(1 - side).wait_recv()

        for h in range(2):
            @pl.when(jnp.logical_and(has[side], jnp.logical_not(pure)))
            def _():
                for f in range(3):
                    raw_copy(1 - side, f, h).wait_recv()

        @pl.when(jnp.logical_and(has[side], pure))
        def _():
            keep = own_cut() < HALF
            for f in range(3):
                y = value(pl.ds(rows + slot_of[side] * edge + f * lat_rows, lat_rows))
                lev_field[side, f] = jnp.where(keep, y, lev_field[side, f])
    for side, l, sign in ((0, 0, QUARTER), (1, levels - 1, -QUARTER)):
        pair = sign * (lev_wind[side] + wind_ref[l])
        for f in range(3):
            outs[f][l] += pair * (lev_field[side, f] + field_ref[f, l])
            result_copy(f, l).start()
    for l in range(levels):
        for f in range(3):
            result_copy(f, l).wait()
    for to in range(2):
        @pl.when(has[to])
        def _():
            wind_copy(to).wait_send()

        @pl.when(jnp.logical_and(has[to], pure))
        def _():
            for i in range(steps):
                spec_copy(to, i).wait_send()

        for h in range(2):
            @pl.when(jnp.logical_and(has[to], jnp.logical_not(pure)))
            def _():
                for f in range(3):
                    raw_copy(to, f, h).wait_send()

        @pl.when(has[2 + to])
        def _():
            lat_copy(to).wait_send()


def store_kernel(in0, in1, in2, out0, out1, out2, held, in_sem, out_sem):
    sources, results = (in0, in1, in2), (out0, out1, out2)
    parts = [(f, l) for l in range(in0.shape[0]) for f in range(3)]
    reads = [pltpu.make_async_copy(sources[f].at[l], held.at[f, l], in_sem.at[f, l]) for f, l in parts]
    writes = [pltpu.make_async_copy(held.at[f, l], results[f].at[l], out_sem.at[f, l]) for f, l in parts]
    for copy in reads:
        copy.start()
    for read, write in zip(reads, writes):
        read.wait()
        write.start()
    for copy in writes:
        copy.wait()


def stored(fields):
    shape = fields[0].shape
    hbm = pl.BlockSpec(memory_space=pl.ANY)
    one = jax.ShapeDtypeStruct(shape, jnp.float32)
    dma = pltpu.SemaphoreType.DMA
    return pl.pallas_call(
        store_kernel, out_shape=(one,) * 3, in_specs=[hbm] * 3, out_specs=(hbm,) * 3,
        scratch_shapes=[pltpu.VMEM((3,) + shape, jnp.float32), dma((3, shape[0])), dma((3, shape[0]))],
        compiler_params=pltpu.CompilerParams(vmem_limit_bytes=58 * 1024 * 1024),
    )(*fields)


def solution(mesh):
    lat_count, lev_count = mesh.shape["lat"], mesh.shape["lev"]

    def on_device(zonal_wind, merid_wind, tracer, vertical_wind, cutoff):
        levels, lat_rows, _ = zonal_wind.shape
        total_rows = lat_rows * lat_count
        cap = total_rows * 40 // 256
        high, low = half_tables()
        steps = high.shape[0]
        edge = 3 * lat_rows
        rows = levels * edge
        wide = rows + edge * (1 if lev_count == 2 else 2)
        vmem = pl.BlockSpec(memory_space=pltpu.VMEM)
        smem = pl.BlockSpec(memory_space=pltpu.SMEM)
        hbm = pl.BlockSpec(memory_space=pl.ANY)
        one = jax.ShapeDtypeStruct(zonal_wind.shape, jnp.float32)
        dma = pltpu.SemaphoreType.DMA
        fields = pl.pallas_call(
            lambda *refs: kernel(lat_count, lev_count, cap, *refs),
            out_shape=(one, one, one),
            in_specs=[hbm] * 4 + [smem, vmem, hbm, hbm],
            out_specs=(hbm,) * 3,
            scratch_shapes=[
                pltpu.VMEM((3, levels, lat_rows, NLON), jnp.float32),
                pltpu.VMEM((levels, lat_rows, NLON), jnp.float32),
                pltpu.VMEM(high.shape, jnp.bfloat16),
                pltpu.VMEM(low.shape, jnp.bfloat16),
                pltpu.VMEM((2, rows, HALF), jnp.bfloat16),
                pltpu.VMEM((2, rows, HALF), jnp.bfloat16),
                pltpu.VMEM((steps, rows, 2 * CHUNK), jnp.float32),
                pltpu.VMEM((2, steps, edge, 2 * CHUNK), jnp.float32),
                pltpu.VMEM((steps, wide, 2 * CHUNK), jnp.bfloat16),
                pltpu.VMEM((steps, wide, 2 * CHUNK), jnp.bfloat16),
                pltpu.VMEM((2, wide, HALF), jnp.float32),
                pltpu.VMEM((2, 3, lat_rows, NLON), jnp.float32),
                pltpu.VMEM((2, lat_rows, NLON), jnp.float32),
                pltpu.VMEM((2, 3 * levels, NLON), jnp.float32),
                pltpu.VMEM((2, 3 * levels, NLON), jnp.float32),
                pltpu.VMEM((3, levels, lat_rows, NLON), jnp.float32),
                dma((4,)), dma((3, levels)), dma((2, steps)), dma((2,)), dma((2,)), dma((2, 3, 2)), dma((2, 3, 2)),
                dma((2, steps)), dma((2, steps)), dma((2,)), dma((2,)),
            ],
            compiler_params=pltpu.CompilerParams(
                collective_id=0, has_side_effects=True, vmem_limit_bytes=58 * 1024 * 1024
            ),
        )(
            zonal_wind, merid_wind, tracer, vertical_wind, cutoff,
            jnp.asarray(latitude_factors(total_rows)), jnp.asarray(high), jnp.asarray(low),
        )
        return stored(fields)

    spec = P("lev", "lat", None)
    return jax.shard_map(
        on_device, mesh=mesh, in_specs=(spec,) * 4 + (P(),), out_specs=(spec,) * 3, check_vma=False
    )
```

```python
import math

import jax
import jax.numpy as jnp
import ml_dtypes
import numpy as np
from jax import lax
from jax.experimental import pallas as pl
from jax.experimental.pallas import tpu as pltpu
from jax.sharding import PartitionSpec as P

NLON = 2880
KMAX = 720
HALF = NLON // 2
CHUNK = 128
MESH = pl.DeviceIdType.MESH
QUARTER = 0.025


def half_tables():
    modes = KMAX // 2
    chunks = -(-modes // CHUNK)
    tables = np.zeros((2, chunks, HALF, 2 * CHUNK), np.float32)
    points = np.arange(HALF, dtype=np.int64)
    for parity in range(2):
        for chunk in range(chunks):
            ids = np.arange(chunk * CHUNK, min((chunk + 1) * CHUNK, modes), dtype=np.int64)
            angles = (points[:, None] * (2 * ids + parity)[None, :] % NLON) * (2.0 * math.pi / NLON)
            tables[parity, chunk, :, : len(ids)] = np.cos(angles)
            tables[parity, chunk, :, CHUNK : CHUNK + len(ids)] = np.sin(angles)
    tables = tables.reshape(2 * chunks, HALF, 2 * CHUNK)
    high = tables.astype(ml_dtypes.bfloat16)
    low = (tables - high.astype(np.float32)).astype(ml_dtypes.bfloat16)
    return high, low


def split(x):
    high = x.astype(jnp.bfloat16)
    return high, (x - high.astype(jnp.float32)).astype(jnp.bfloat16)


def dot(a, b, transposed=False):
    dims = (((1,), (1 if transposed else 0,)), ((), ()))
    return lax.dot_general(a, b, dims, preferred_element_type=jnp.float32)


def latitude_factors(total_rows):
    ids = np.arange(total_rows + 1, dtype=np.float64)
    face = np.sin(ids * (math.pi / total_rows))
    center = np.sin((ids[:-1] + 0.5) * (math.pi / total_rows))
    return np.stack(
        [QUARTER * face[:-1] / center, QUARTER * face[1:] / center, QUARTER / center], axis=1
    ).astype(np.float32)


def east_of(x):
    return jnp.concatenate([x[:, 1:], x[:, :1]], axis=1)


def west_of(x):
    return jnp.concatenate([x[:, -1:], x[:, :-1]], axis=1)


def kernel(
    lat_count, lev_count, cap, zonal_in, merid_in, tracer_in, wind_in, cut_ref, factor_ref, high_in, low_in,
    out0, out1, out2,
    field_ref, wind_ref, high_ref, low_ref, xh, xl, spec, spec_in, sh, sl, acc,
    lev_field, lev_wind, lat_out, lat_in, out_ref,
    load_sem, out_sem, table_sem, wind_send, wind_recv, raw_send, raw_recv, spec_send, spec_recv, lat_send, lat_recv,
):
    lat, lev = lax.axis_index("lat"), lax.axis_index("lev")
    inputs = (zonal_in, merid_in, tracer_in)
    results = (out0, out1, out2)
    outs = (out_ref.at[0], out_ref.at[1], out_ref.at[2])
    levels, lat_rows = wind_ref.shape[0], wind_ref.shape[1]
    steps = high_ref.shape[0]
    chunks = steps // 2
    edge = 3 * lat_rows
    rows = levels * edge
    half = lat_rows // 2
    total_rows = lat_count * lat_rows
    has = (lev > 0, lev < lev_count - 1, lat > 0, lat < lat_count - 1)
    there = ((lat, lev - 1), (lat, lev + 1), (lat - 1, lev), (lat + 1, lev))
    slots = 1 if lev_count == 2 else 2
    slot_of = (0, slots - 1)
    first_row = lat * lat_rows

    def spans(start, count):
        some = jnp.logical_or(start < cap, start + count > total_rows - cap)
        inside = jnp.logical_and(start + count > cap, start < total_rows - cap)
        return some, inside

    filtered, _ = spans(first_row, lat_rows)
    mixed = jnp.logical_and(filtered, spans(first_row, lat_rows)[1])
    pure = jnp.logical_and(filtered, jnp.logical_not(mixed))
    early = tuple(jnp.logical_not(spans(first_row + h * half, half)[0]) for h in range(2))
    late = tuple(jnp.logical_and(mixed, jnp.logical_not(early[h])) for h in range(2))

    def result_copy(f, l):
        return pltpu.make_async_copy(out_ref.at[f, l], results[f].at[l], out_sem.at[f, l])

    barrier = pltpu.get_barrier_semaphore()
    for side in range(4):
        @pl.when(has[side])
        def _():
            pl.semaphore_signal(barrier, inc=1, device_id=there[side], device_id_type=MESH)

    loads = [pltpu.make_async_copy(inputs[f], field_ref.at[f], load_sem.at[f]) for f in range(3)]
    load_wind = pltpu.make_async_copy(wind_in, wind_ref, load_sem.at[3])
    for copy in loads:
        copy.start()

    def table_loads(i):
        return (
            pltpu.make_async_copy(high_in.at[i], high_ref.at[i], table_sem.at[0, i]),
            pltpu.make_async_copy(low_in.at[i], low_ref.at[i], table_sem.at[1, i]),
        )

    @pl.when(filtered)
    def _():
        for i in range(steps):
            for copy in table_loads(i):
                copy.start()

    load_wind.start()
    pl.semaphore_wait(barrier, sum(side.astype(jnp.int32) for side in has))

    def remote(source, target, send, recv, to):
        return pltpu.make_async_remote_copy(
            src_ref=source, dst_ref=target, send_sem=send, recv_sem=recv,
            device_id=there[to], device_id_type=MESH,
        )

    edge_level = (0, levels - 1)

    def wind_copy(to):
        return remote(
            wind_in.at[edge_level[to]], lev_wind.at[1 - to], wind_send.at[to], wind_recv.at[1 - to], to
        )

    def raw_copy(to, f, h, source=inputs):
        span = pl.ds(h * half, half)
        return remote(
            source[f].at[edge_level[to], span], lev_field.at[1 - to, f, span],
            raw_send.at[to, f, h], raw_recv.at[1 - to, f, h], to,
        )

    def spec_copy(to, i):
        return remote(
            spec.at[i, pl.ds(edge_level[to] * edge, edge)], spec_in.at[1 - to, i],
            spec_send.at[to, i], spec_recv.at[1 - to, i], to,
        )

    def lat_copy(to):
        return remote(lat_out.at[to], lat_in.at[1 - to], lat_send.at[to], lat_recv.at[1 - to], 2 + to)

    for to in range(2):
        for h in range(2):
            @pl.when(jnp.logical_and(has[to], early[h]))
            def _():
                for f in range(3):
                    raw_copy(to, f, h).start()

        @pl.when(jnp.logical_and(has[to], jnp.logical_not(pure)))
        def _():
            wind_copy(to).start()

    for side in range(2):
        @pl.when(jnp.logical_or(jnp.logical_not(has[side]), pure))
        def _():
            lev_field[side] = jnp.zeros(lev_field.shape[1:], jnp.float32)

        @pl.when(jnp.logical_not(has[side]))
        def _():
            lev_wind[side] = jnp.zeros(lev_wind.shape[1:], jnp.float32)

        @pl.when(jnp.logical_not(has[2 + side]))
        def _():
            lat_in[side] = jnp.zeros(lat_in.shape[1:], jnp.float32)

    row = lax.broadcasted_iota(jnp.int32, (lat_rows, 1), 0)
    for copy in loads:
        copy.wait()

    def own_cut():
        cut = jnp.zeros((lat_rows, 1), jnp.int32)
        for j in range(lat_rows):
            cut = jnp.where(row == j, cut_ref[first_row + j], cut)
        return cut

    def value(at):
        even, odd = acc[0, at, :], acc[1, at, :]
        return jnp.concatenate([even + odd, even - odd], axis=1)

    @pl.when(filtered)
    def _():
        cut = own_cut()

        for l in range(levels):
            for f in range(3):
                x = field_ref[f, l]
                first, second = x[:, :HALF], x[:, HALF:]
                at = pl.ds(l * edge + f * lat_rows, lat_rows)
                for p, folded in enumerate((first + second, first - second)):
                    high, low = split(folded)
                    xh[p, at, :] = high
                    xl[p, at, :] = low

        def forward(i, carry):
            parity, chunk = i // chunks, i % chunks
            for copy in table_loads(i):
                copy.wait()
            th, tl = high_ref[i], low_ref[i]
            part = dot(xh[parity], th) + dot(xl[parity], th) + dot(xh[parity], tl)
            lane = lax.broadcasted_iota(jnp.int32, (lat_rows, 2 * CHUNK), 1) % CHUNK
            mode = 2 * (chunk * CHUNK + lane) + parity
            weight = jnp.where(mode == 0, jnp.float32(1.0 / NLON), jnp.float32(2.0 / NLON))
            weight = jnp.where(mode <= cut, weight, 0.0)
            part = part * jnp.concatenate([weight] * (3 * levels), axis=0)
            spec[i] = part
            for to in range(2):
                @pl.when(jnp.logical_and(has[to], pure))
                def _():
                    spec_copy(to, i).start()
            high, low = split(part)
            sh[i, pl.ds(0, rows), :] = high
            sl[i, pl.ds(0, rows), :] = low
            return carry

        lax.fori_loop(0, steps, forward, 0)
        for to in range(2):
            @pl.when(jnp.logical_and(has[to], pure))
            def _():
                wind_copy(to).start()

        def backward(i, carry):
            parity, chunk = i // chunks, i % chunks
            for side in range(2):
                at = pl.ds(rows + slot_of[side] * edge, edge)

                @pl.when(jnp.logical_and(has[side], pure))
                def _():
                    spec_copy(1 - side, i).wait_recv()
                    high, low = split(spec_in[side, i])
                    sh[i, at, :] = high
                    sl[i, at, :] = low

                empty = jnp.logical_not(jnp.logical_and(has[side], pure)) if slots == 2 else mixed

                @pl.when(empty)
                def _():
                    sh[i, at, :] = jnp.zeros((edge, 2 * CHUNK), jnp.bfloat16)
                    sl[i, at, :] = jnp.zeros((edge, 2 * CHUNK), jnp.bfloat16)

            th, tl = high_ref[i], low_ref[i]

            def inverse(count):
                at = pl.ds(0, count)
                high, low = sh[i, at, :], sl[i, at, :]
                part = dot(high, th, True) + dot(low, th, True) + dot(high, tl, True)

                @pl.when(chunk == 0)
                def _():
                    acc[parity, at, :] = part

                @pl.when(chunk > 0)
                def _():
                    acc[parity, at, :] += part

            @pl.when(pure)
            def _():
                inverse(sh.shape[1])

            @pl.when(mixed)
            def _():
                inverse(rows)

            return carry

        lax.fori_loop(0, steps, backward, 0)
        keep = cut < HALF

        for l in range(levels):
            for f in range(3):
                y = value(pl.ds(l * edge + f * lat_rows, lat_rows))
                field_ref[f, l] = jnp.where(keep, y, field_ref[f, l])

    for to in range(2):
        for h in range(2):
            @pl.when(jnp.logical_and(has[to], late[h]))
            def _():
                for f in range(3):
                    raw_copy(to, f, h, (field_ref.at[0], field_ref.at[1], field_ref.at[2])).start()

    for to, at in ((0, 0), (1, lat_rows - 1)):
        for f in range(3):
            for l in range(levels):
                lat_out[to, f * levels + l : f * levels + l + 1, :] = field_ref[f, l, at : at + 1, :]

        @pl.when(has[2 + to])
        def _():
            lat_copy(to).start()

    load_wind.wait()
    factors = factor_ref[pl.ds(pl.multiple_of(first_row, lat_rows), lat_rows), :]
    low_face = jnp.where(row > 0, factors[:, 0:1], 0.0)
    high_face = jnp.where(row < lat_rows - 1, factors[:, 1:2], 0.0)
    zonal_factor = factors[:, 2:3]

    def inner(l, carry):
        below, above = jnp.maximum(l - 1, 0), jnp.minimum(l + 1, levels - 1)
        zonal = field_ref[0, l]
        merid = field_ref[1, l]
        wind_here = wind_ref[l]
        east_wind = (zonal + east_of(zonal)) * zonal_factor
        merid_pair = merid + jnp.roll(merid, 1, axis=0)
        low_wind = jnp.where(l > 0, jnp.float32(QUARTER), 0.0) * (wind_ref[below] + wind_here)
        high_wind = jnp.where(l < levels - 1, jnp.float32(QUARTER), 0.0) * (wind_here + wind_ref[above])
        for f in range(3):
            x = field_ref[f, l]
            flux_x = east_wind * (x + east_of(x))
            flux_y = merid_pair * (x + jnp.roll(x, 1, axis=0))
            div_y = high_face * jnp.roll(flux_y, -1, axis=0) - low_face * flux_y
            div_z = high_wind * (x + field_ref[f, above]) - low_wind * (field_ref[f, below] + x)
            outs[f][l] = x - (flux_x - west_of(flux_x)) - div_y - div_z
        return carry

    lax.fori_loop(0, levels, inner, 0)

    for side in range(2):
        @pl.when(has[2 + side])
        def _():
            lat_copy(1 - side).wait_recv()
    for side, at, factor in ((0, 0, factors[0:1, 0:1]), (1, lat_rows - 1, -factors[lat_rows - 1 :, 1:2])):
        for l in range(levels):
            own = pl.ds(at, 1)
            pair = factor * (lat_in[side, levels + l : levels + l + 1, :] + field_ref[1, l, own, :])
            for f in range(3):
                halo = lat_in[side, f * levels + l : f * levels + l + 1, :]
                outs[f][l, own, :] += pair * (halo + field_ref[f, l, own, :])
    for l in range(1, levels - 1):
        for f in range(3):
            result_copy(f, l).start()

    for side in range(2):
        @pl.when(has[side])
        def _():
            wind_copy(1 - side).wait_recv()

        for h in range(2):
            @pl.when(jnp.logical_and(has[side], jnp.logical_not(pure)))
            def _():
                for f in range(3):
                    raw_copy(1 - side, f, h).wait_recv()

        @pl.when(jnp.logical_and(has[side], pure))
        def _():
            keep = own_cut() < HALF
            for f in range(3):
                y = value(pl.ds(rows + slot_of[side] * edge + f * lat_rows, lat_rows))
                lev_field[side, f] = jnp.where(keep, y, lev_field[side, f])
    for side, l, sign in ((0, 0, QUARTER), (1, levels - 1, -QUARTER)):
        pair = sign * (lev_wind[side] + wind_ref[l])
        for f in range(3):
            outs[f][l] += pair * (lev_field[side, f] + field_ref[f, l])
            result_copy(f, l).start()
    for l in range(levels):
        for f in range(3):
            result_copy(f, l).wait()
    for to in range(2):
        @pl.when(has[to])
        def _():
            wind_copy(to).wait_send()

        @pl.when(jnp.logical_and(has[to], pure))
        def _():
            for i in range(steps):
                spec_copy(to, i).wait_send()

        for h in range(2):
            @pl.when(jnp.logical_and(has[to], jnp.logical_not(pure)))
            def _():
                for f in range(3):
                    raw_copy(to, f, h).wait_send()

        @pl.when(has[2 + to])
        def _():
            lat_copy(to).wait_send()


def store_kernel(in0, in1, in2, out0, out1, out2, held, in_sem, out_sem):
    sources, results = (in0, in1, in2), (out0, out1, out2)
    parts = [(f, l) for l in range(in0.shape[0]) for f in range(3)]
    reads = [pltpu.make_async_copy(sources[f].at[l], held.at[f, l], in_sem.at[f, l]) for f, l in parts]
    writes = [pltpu.make_async_copy(held.at[f, l], results[f].at[l], out_sem.at[f, l]) for f, l in parts]
    for copy in reads:
        copy.start()
    for read, write in zip(reads, writes):
        read.wait()
        write.start()
    for copy in writes:
        copy.wait()


def stored(fields):
    shape = fields[0].shape
    hbm = pl.BlockSpec(memory_space=pl.ANY)
    one = jax.ShapeDtypeStruct(shape, jnp.float32)
    dma = pltpu.SemaphoreType.DMA
    return pl.pallas_call(
        store_kernel, out_shape=(one,) * 3, in_specs=[hbm] * 3, out_specs=(hbm,) * 3,
        scratch_shapes=[pltpu.VMEM((3,) + shape, jnp.float32), dma((3, shape[0])), dma((3, shape[0]))],
        compiler_params=pltpu.CompilerParams(vmem_limit_bytes=58 * 1024 * 1024),
    )(*fields)


def solution(mesh):
    lat_count, lev_count = mesh.shape["lat"], mesh.shape["lev"]

    def on_device(zonal_wind, merid_wind, tracer, vertical_wind, cutoff):
        levels, lat_rows, _ = zonal_wind.shape
        total_rows = lat_rows * lat_count
        cap = total_rows * 40 // 256
        high, low = half_tables()
        steps = high.shape[0]
        edge = 3 * lat_rows
        rows = levels * edge
        wide = rows + edge * (1 if lev_count == 2 else 2)
        vmem = pl.BlockSpec(memory_space=pltpu.VMEM)
        smem = pl.BlockSpec(memory_space=pltpu.SMEM)
        hbm = pl.BlockSpec(memory_space=pl.ANY)
        one = jax.ShapeDtypeStruct(zonal_wind.shape, jnp.float32)
        dma = pltpu.SemaphoreType.DMA
        fields = pl.pallas_call(
            lambda *refs: kernel(lat_count, lev_count, cap, *refs),
            out_shape=(one, one, one),
            in_specs=[hbm] * 4 + [smem, vmem, hbm, hbm],
            out_specs=(hbm,) * 3,
            scratch_shapes=[
                pltpu.VMEM((3, levels, lat_rows, NLON), jnp.float32),
                pltpu.VMEM((levels, lat_rows, NLON), jnp.float32),
                pltpu.VMEM(high.shape, jnp.bfloat16),
                pltpu.VMEM(low.shape, jnp.bfloat16),
                pltpu.VMEM((2, rows, HALF), jnp.bfloat16),
                pltpu.VMEM((2, rows, HALF), jnp.bfloat16),
                pltpu.VMEM((steps, rows, 2 * CHUNK), jnp.float32),
                pltpu.VMEM((2, steps, edge, 2 * CHUNK), jnp.float32),
                pltpu.VMEM((steps, wide, 2 * CHUNK), jnp.bfloat16),
                pltpu.VMEM((steps, wide, 2 * CHUNK), jnp.bfloat16),
                pltpu.VMEM((2, wide, HALF), jnp.float32),
                pltpu.VMEM((2, 3, lat_rows, NLON), jnp.float32),
                pltpu.VMEM((2, lat_rows, NLON), jnp.float32),
                pltpu.VMEM((2, 3 * levels, NLON), jnp.float32),
                pltpu.VMEM((2, 3 * levels, NLON), jnp.float32),
                pltpu.VMEM((3, levels, lat_rows, NLON), jnp.float32),
                dma((4,)), dma((3, levels)), dma((2, steps)), dma((2,)), dma((2,)), dma((2, 3, 2)), dma((2, 3, 2)),
                dma((2, steps)), dma((2, steps)), dma((2,)), dma((2,)),
            ],
            compiler_params=pltpu.CompilerParams(
                collective_id=0, has_side_effects=True, vmem_limit_bytes=58 * 1024 * 1024
            ),
        )(
            zonal_wind, merid_wind, tracer, vertical_wind, cutoff,
            jnp.asarray(latitude_factors(total_rows)), jnp.asarray(high), jnp.asarray(low),
        )
        return stored(fields)

    spec = P("lev", "lat", None)
    return jax.shard_map(
        on_device, mesh=mesh, in_specs=(spec,) * 4 + (P(),), out_specs=(spec,) * 3, check_vma=False
    )
```
